256 devices in a mesh: head: 8 (over z), inner: 4 (over x_hi, core), outer: 8 (over x_lo, y).
Axes of the slice: x: 4 (x_hi: 2, x_lo: 2; x = x_hi * 2 + x_lo), y: 4, z: 8, core: 2. Of those that a mesh axis runs over, the one named last changes fastest.
Arguments:
- queries: bfloat16 [32, 1024, 4096], P(('inner', 'outer'), None, 'head'), may hold values from -12.5 to 12.5
- keys: bfloat16 [32, 1024, 1024], P(('inner', 'outer'), 'head'), may hold values from -12.5 to 12.5
- values: bfloat16 [32, 1024, 1024], P(('inner', 'outer'), 'head'), may hold values from -5 to 5
- span_order: int32 [32], replicated, may hold values from 0 to 31, each once
- prev_out: bfloat16 [32, 1024, 4096], P(('inner', 'outer'), None, 'head'), may hold values from -4 to 4
- earlier_log_total: float32 [32, 32, 1024], P(('inner', 'outer'), 'head'), may hold values from 6 to 12
Outputs:
- attn_out: bfloat16 [32, 1024, 4096], P(('inner', 'outer'), None, 'head')
- attn_lse: float32 [32, 32, 1024], P(('inner', 'outer'), 'head')
The draws below stay inside these ranges and needn't reach their ends.
All inputs are finite; a program needn't handle non-finite values.
Results may differ from the reference program's by a relative error of at most 0.002.
Values may be sent and summed in bfloat16 or wider, within the bound.
A program may use at most 192 MiB of HBM per device.

```python
import math
import jax
import jax.numpy as jnp
from jax import lax

QUERY_HEADS = 32
KEY_VALUE_HEADS = 8
HEAD_WIDTH = 128
VISIBLE_BLOCKS = 4
STRIDE = 8
CONTEXT_BLOCKS = 32
BLOCK_ROWS = 1024
HALF = 512


def draw_queries(key, part):
    key = jax.random.fold_in(key, 11)
    base_key = jax.random.fold_in(key, 0)
    complete_shape = (CONTEXT_BLOCKS, BLOCK_ROWS, QUERY_HEADS, HEAD_WIDTH)
    base_sample = jnp.clip(1.5 * jax.random.normal(base_key, complete_shape, jnp.float32), -6.0, 6.0)
    return base_sample.reshape(CONTEXT_BLOCKS, BLOCK_ROWS, QUERY_HEADS * HEAD_WIDTH).astype(jnp.bfloat16)


def draw_keys(key, part):
    key = jax.random.fold_in(key, 12)
    base_key = jax.random.fold_in(key, 0)
    complete_shape = (CONTEXT_BLOCKS, BLOCK_ROWS, KEY_VALUE_HEADS, HEAD_WIDTH)
    base_sample = jnp.clip(1.5 * jax.random.normal(base_key, complete_shape, jnp.float32), -6.0, 6.0)
    return base_sample.reshape(CONTEXT_BLOCKS, BLOCK_ROWS, KEY_VALUE_HEADS * HEAD_WIDTH).astype(jnp.bfloat16)


def steps_of(stream_key, extent, cuts, low, top_value):
    gain, own = 1.0, jax.random.fold_in(stream_key, 6)
    for axis_at, parts in cuts:
        steps = jnp.exp(jax.random.uniform(jax.random.fold_in(own, axis_at), (parts,), jnp.float32, low / len(cuts), top_value / len(cuts)))
        gain = gain * jnp.repeat(steps, extent[axis_at] // parts).reshape([-1 if axis == axis_at else 1 for axis in range(len(extent))])
    return gain


def scatter_about(stream_key, dims, scale, bound, cuts=(), held_as=jnp.bfloat16):
    drawn = jax.random.normal(stream_key, dims, jnp.float32) * scale
    if len(cuts) > 0:
        drawn = steps_of(stream_key, dims, cuts, -0.22, 0.18) * drawn
    return jnp.clip(drawn, min=-bound, max=bound).astype(held_as)


def setup_inputs(seed: int = 0) -> dict:
    key_of = jax.random.split(jax.random.key(seed), 7)
    return {
        "queries": draw_queries(jax.random.fold_in(key_of[6], 71), 0),
        "keys": draw_keys(jax.random.fold_in(key_of[6], 71), 0),
        "values": scatter_about(key_of[2], (CONTEXT_BLOCKS, BLOCK_ROWS, KEY_VALUE_HEADS * HEAD_WIDTH), 1.0, 5.0, ((0, 32), (1, 8))),
        "span_order": jax.random.permutation(key_of[3], CONTEXT_BLOCKS).astype(jnp.int32),
        "prev_out": scatter_about(key_of[4], (CONTEXT_BLOCKS, BLOCK_ROWS, QUERY_HEADS * HEAD_WIDTH), 0.7, 4.0, ((0, 32), (2, 8))),
        "earlier_log_total": jnp.clip(6.0 + 6.0 * jax.random.uniform(key_of[5], (CONTEXT_BLOCKS, QUERY_HEADS, BLOCK_ROWS), jnp.float32) ** steps_of(key_of[5], (CONTEXT_BLOCKS, QUERY_HEADS, BLOCK_ROWS), ((0, 32), (1, 8)), -0.2, 0.2), 6.0, 12.0),
    }


def span_positions(span_order, block_lookup, row_ids, half_rows):
    block_count = span_order.shape[0]
    first_span = jnp.sum(jnp.where(jnp.arange(block_count, dtype=jnp.int32) == block_lookup, span_order, 0))
    span_at = jnp.where(row_ids < half_rows, first_span, 2 * block_count - 1 - first_span)
    return (span_at * half_rows + row_ids % half_rows).astype(jnp.int32)

def reference(queries, keys, values, span_order, prev_out, earlier_log_total):
    row_ids = jnp.arange(BLOCK_ROWS, dtype=jnp.int32)
    group_width = QUERY_HEADS // KEY_VALUE_HEADS
    inv_scale = 1.0 / math.sqrt(HEAD_WIDTH)

    def one_block(block_lookup):
        source_outer = (block_lookup % STRIDE + STRIDE - 1) % STRIDE
        source_blocks = (jnp.arange(VISIBLE_BLOCKS, dtype=jnp.int32) * STRIDE + source_outer).astype(jnp.int32)
        key_pos = jnp.concatenate([span_positions(span_order, source_blocks[cycle_at], row_ids, HALF) for cycle_at in range(VISIBLE_BLOCKS)])
        query_pos = span_positions(span_order, block_lookup, row_ids, HALF)
        allowed = key_pos[None, :] <= query_pos[:, None]
        keys_of_block = jnp.take(keys, source_blocks, axis=0).reshape(VISIBLE_BLOCKS * BLOCK_ROWS, KEY_VALUE_HEADS, HEAD_WIDTH).astype(jnp.float32).transpose(1, 0, 2)
        values_of_block = jnp.take(values, source_blocks, axis=0).reshape(VISIBLE_BLOCKS * BLOCK_ROWS, KEY_VALUE_HEADS, HEAD_WIDTH).astype(jnp.float32).transpose(1, 0, 2)
        queries_of_block = lax.dynamic_index_in_dim(queries, block_lookup, 0, keepdims=False)
        queries_of_block = queries_of_block.reshape(BLOCK_ROWS, KEY_VALUE_HEADS, group_width, HEAD_WIDTH).astype(jnp.float32).transpose(1, 2, 0, 3)
        block_earlier = lax.dynamic_index_in_dim(prev_out, block_lookup, 0, keepdims=False)
        block_earlier = block_earlier.reshape(BLOCK_ROWS, KEY_VALUE_HEADS, group_width, HEAD_WIDTH).astype(jnp.float32).transpose(1, 2, 0, 3)
        block_log_total = lax.dynamic_index_in_dim(earlier_log_total, block_lookup, 0, keepdims=False).reshape(KEY_VALUE_HEADS, group_width, BLOCK_ROWS)

        def one_head(head_parts):
            head_query, head_keys, head_values, head_prev, head_lse = head_parts
            scores = jnp.einsum('grd,kd->grk', head_query, head_keys) * inv_scale
            masked = jnp.where(allowed[None], scores, -jnp.inf)
            peak = jnp.maximum(head_lse, lax.optimization_barrier(jnp.max(masked, axis=-1)))
            weights = jnp.exp(masked - peak[..., None])
            carried = jnp.exp(head_lse - peak)
            total = carried + lax.optimization_barrier(jnp.sum(weights, axis=-1))
            rounded = lax.optimization_barrier(weights.astype(jnp.bfloat16)).astype(jnp.float32)
            mixed_out = head_prev * carried[..., None] + jnp.einsum('grk,kd->grd', rounded, head_values)
            return ((mixed_out / total[..., None]).astype(jnp.bfloat16), peak + jnp.log(total))
        mixed_out, head_lse = lax.map(one_head, (queries_of_block, keys_of_block, values_of_block, block_earlier, block_log_total))
        return (mixed_out.transpose(2, 0, 1, 3).reshape(BLOCK_ROWS, QUERY_HEADS * HEAD_WIDTH), head_lse.reshape(QUERY_HEADS, BLOCK_ROWS))
    attn_out, attn_lse = lax.map(one_block, jnp.arange(CONTEXT_BLOCKS, dtype=jnp.int32))
    return (attn_out, attn_lse)
```

```python
import math

import jax
import jax.numpy as jnp
from jax import lax
from jax.experimental import pallas as pl
from jax.experimental.pallas import tpu as pltpu
from jax.sharding import PartitionSpec as P

MESH = pl.DeviceIdType.MESH
BF16, F32 = jnp.bfloat16, jnp.float32
WIDTH = 128
HALF = 512
HEADS = 4
SLOTS = 4
RELAY = 4
PIECES = 8
PARTS = 2
ROWS = WIDTH // PARTS
SPAN = HALF // PARTS
WAVES = 2 * PARTS
LOG2E = math.log2(math.e)
SCALE2 = LOG2E / math.sqrt(WIDTH)
NT = (((1,), (1,)), ((), ()))
ORDER = (0, 1, 7, 2, 6, 3, 5, 4)


def device(x, y, z, core):
    return {"head": z, "inner": (x // 2) * 2 + core, "outer": (x % 2) * 4 + y}


def kernel(
    span_ref, q_hbm, k_hbm, v_hbm, prev_hbm, lse_ref, out_ref, lse_out_ref,
    w0, w1, w2, w3, q_ref, prev_ref, scores, peak, carry, mixed, totals, vb, lse_cols,
    recv_sem, send_sem, local_sem,
):
    waves = (w0, w1, w2, w3)
    z, inner, outer = lax.axis_index("head"), lax.axis_index("inner"), lax.axis_index("outer")
    core = inner % 2
    x, y = (inner // 2) * 2 + outer // 4, outer % 4
    wrap = y == 0
    sibling = device(x, y, z, 1 - core)
    up = device((x + jnp.where(wrap, 1, 2)) % 4, y, z, core)
    down = device((x + 3) % 4, y, z, core)

    loads = (
        pltpu.make_async_copy(q_hbm.at[0], q_ref, local_sem.at[0]),
        pltpu.make_async_copy(prev_hbm.at[0], prev_ref, local_sem.at[1]),
    )
    for load in loads:
        load.start()

    barrier = pltpu.get_barrier_semaphore()

    def greet(to):
        pl.semaphore_signal(barrier, inc=1, device_id=to, device_id_type=MESH)

    for r in ORDER[::-1]:
        greet(device(x, (y + 3) % 4, (z + 8 - r) % 8, core))
    greet(up)
    greet(sibling)

    @pl.when(wrap)
    def _():
        greet(down)

    pl.semaphore_wait(barrier, PIECES + 2 + jnp.where(wrap, 1, 0))

    def remote(source, target, send, recv, to):
        return pltpu.make_async_remote_copy(
            src_ref=source, dst_ref=target, send_sem=send, recv_sem=recv, device_id=to, device_id_type=MESH
        )

    def landed(w, kind, slot):
        whole = waves[w].at[slot]
        return remote(whole, whole, send_sem.at[w, kind], recv_sem.at[w, kind], sibling)

    def send_out(w):
        source, part = (k_hbm, v_hbm)[w // PARTS], w % PARTS
        slot = jnp.where(y == 3, RELAY, 0)
        rows = pl.ds(pl.multiple_of(z * ROWS, ROWS), ROWS)
        for r in ORDER:
            z_to = (z + r) % 8
            columns = pl.ds(pl.multiple_of(z_to * WIDTH, WIDTH), WIDTH)
            remote(
                source.at[0, part * ROWS : (part + 1) * ROWS, columns], waves[w].at[slot, rows, :],
                send_sem.at[w, 0], recv_sem.at[w, 0], device(x, (y + 1) % 4, z_to, core),
            ).start()

    def spread(w):
        landed(w, 0, 0).wait_recv()

        @pl.when(wrap)
        def _():
            remote(waves[w].at[RELAY], waves[w].at[0], send_sem.at[w, 1], recv_sem.at[w, 1], up).start()
            remote(waves[w].at[RELAY], waves[w].at[1], send_sem.at[w, 2], recv_sem.at[w, 2], down).start()

        @pl.when(jnp.logical_not(wrap))
        def _():
            remote(waves[w].at[0], waves[w].at[1], send_sem.at[w, 2], recv_sem.at[w, 2], up).start()

    def share_first(w):
        @pl.when(wrap)
        def _():
            landed(w, 1, 0).wait_recv()

        remote(waves[w].at[0], waves[w].at[2], send_sem.at[w, 3], recv_sem.at[w, 3], sibling).start()

    def share_second(w):
        landed(w, 2, 1).wait_recv()
        remote(waves[w].at[1], waves[w].at[3], send_sem.at[w, 4], recv_sem.at[w, 4], sibling).start()

    def shared(w, slot):
        landed(w, slot + 1, slot).wait_recv()

    for w in range(WAVES):
        send_out(w)

    peak[...] = jnp.full(peak.shape, -jnp.inf, F32)
    for chunk in range(2 * HALF // WIDTH):
        half, low = chunk // 4, (chunk % 4) * WIDTH
        for h in range(HEADS):
            row = lse_ref[0, h : h + 1, chunk * WIDTH : (chunk + 1) * WIDTH] * LOG2E
            carry[half, h, low : low + WIDTH, :] = jnp.broadcast_to(row, (WIDTH, WIDTH)).T

    own_span = span_ref[inner * 8 + outer]
    first = jnp.where(wrap, (x + 3) % 4, x) // 2
    is_low = []
    for hi, at_core in ((first, core), (1 - first, core), (first, 1 - core), (1 - first, 1 - core)):
        is_low.append(span_ref[(hi * 2 + at_core) * 8 + (outer + 7) % 8] < own_span)
    loads[0].wait()

    def score(part, slot):
        found = waves[part]
        low_keys = found[slot, 0:SPAN, :]
        either_keys = jnp.where(is_low[slot], low_keys, found[slot, SPAN : 2 * SPAN, :])
        at = (part * SLOTS + slot) * 2
        for h in range(HEADS):
            columns = slice(h * WIDTH, (h + 1) * WIDTH)
            high = q_ref[HALF : 2 * HALF, columns]
            either = jnp.where(is_low[slot], q_ref[0:HALF, columns], high)
            tops = []
            for n, (query, key) in enumerate(((high, low_keys), (either, either_keys))):
                got = lax.dot_general(query, key, NT, preferred_element_type=F32)
                scores[at + n, h] = got
                top = got[:, 0:WIDTH]
                for low in range(WIDTH, SPAN, WIDTH):
                    top = jnp.maximum(top, got[:, low : low + WIDTH])
                tops.append(top)
            peak[0, h] = jnp.maximum(peak[0, h], jnp.where(is_low[slot], tops[1], -jnp.inf))
            peak[1, h] = jnp.maximum(
                jnp.maximum(peak[1, h], tops[0]), jnp.where(is_low[slot], -jnp.inf, tops[1])
            )

    def masked_values(part):
        found = waves[PARTS + part]
        for slot in range(SLOTS):
            low_values, high_values = found[slot, 0:SPAN, :], found[slot, SPAN : 2 * SPAN, :]
            nothing = jnp.zeros_like(low_values)
            vb[part * SLOTS + slot, :, 0:WIDTH] = jnp.where(is_low[slot], low_values, nothing)
            vb[part * SLOTS + slot, :, WIDTH : 2 * WIDTH] = jnp.where(is_low[slot], nothing, high_values)

    def weigh(at, h, top):
        total, parts = None, []
        for low in range(0, SPAN, WIDTH):
            weight = jnp.exp2(scores[at, h, :, low : low + WIDTH] * SCALE2 - top)
            total = weight if total is None else total + weight
            parts.append(weight.astype(BF16))
        return jnp.concatenate(parts, axis=1), total

    def mix(part, h):
        tops = (peak[0, h], peak[1, h])
        low_total = high_total = high_mix = both = None

        def add(total, more):
            return more if total is None else total + more

        for slot in range(SLOTS):
            at = part * SLOTS + slot
            weights, total = weigh(2 * at, h, tops[1])
            high_total = add(high_total, total)
            high_mix = add(high_mix, jnp.dot(weights, waves[PARTS + part][slot, 0:SPAN, :], preferred_element_type=F32))
            weights, total = weigh(2 * at + 1, h, jnp.where(is_low[slot], tops[0], tops[1]))
            both = add(both, jnp.dot(weights, vb[at], preferred_element_type=F32))
            low_total = add(low_total, jnp.where(is_low[slot], total, 0.0))
            high_total = add(high_total, jnp.where(is_low[slot], 0.0, total))
        return (low_total, high_total), (both[:, 0:WIDTH], high_mix + both[:, WIDTH : 2 * WIDTH])

    lane = lax.broadcasted_iota(jnp.int32, (HALF, WIDTH), 1)

    def mix_first(h):
        got_totals, got = mix(0, h)
        for half in range(2):
            totals[half, h] = got_totals[half]
            mixed[half, h] = got[half]

    def mix_last(h):
        columns = pl.ds(pl.multiple_of(h * WIDTH, WIDTH), WIDTH)
        got_totals, got = mix(1, h)
        for half in range(2):
            own = slice(half * HALF, (half + 1) * HALF)
            top = peak[half, h]
            kept = jnp.exp2(carry[half, h] - top)
            total = jnp.sum(totals[half, h] + got_totals[half], axis=1, keepdims=True)
            total = jnp.broadcast_to(total, (HALF, WIDTH)) + kept
            result = (prev_ref[own, columns].astype(F32) * kept + (mixed[half, h] + got[half])) / total
            out_ref[0, own, columns] = result.astype(BF16)
            log_total = top * (1.0 / LOG2E) + jnp.log(total)
            lse_cols[own, :] = jnp.where(lane == h, log_total, lse_cols[own, :])

    def two(step, n):
        def run(at, _):
            step(n + 2 * at)
            step(n + 2 * at + 1)
            return 0

        return run

    spread(0)
    share_first(0)
    score(0, 0)
    shared(0, 2)
    score(0, 2)
    spread(1)
    share_second(0)
    share_first(1)
    score(0, 1)
    score(1, 0)
    shared(0, 3)
    score(0, 3)
    spread(2)
    share_second(1)
    share_first(2)
    shared(1, 2)
    score(1, 2)
    score(1, 1)
    shared(1, 3)
    score(1, 3)
    spread(3)
    share_second(2)
    share_first(3)
    for half in range(2):
        for h in range(HEADS):
            top = jnp.max(peak[half, h], axis=1, keepdims=True) * SCALE2
            peak[half, h] = jnp.maximum(jnp.broadcast_to(top, (HALF, WIDTH)), carry[half, h])
    shared(2, 2)
    shared(2, 3)
    masked_values(0)
    lax.fori_loop(0, 1, two(mix_first, 0), 0)
    share_second(3)
    lax.fori_loop(0, 1, two(mix_first, 2), 0)
    shared(3, 2)
    shared(3, 3)
    masked_values(1)
    loads[1].wait()
    lse_cols[...] = jnp.zeros(lse_cols.shape, F32)
    lax.fori_loop(0, HEADS // 2, two(mix_last, 0), 0)
    for chunk in range(2 * HALF // WIDTH):
        own = slice(chunk * WIDTH, (chunk + 1) * WIDTH)
        lse_out_ref[0, :, own] = lse_cols[own, :].T[0:HEADS, :]

    for w in range(WAVES):
        for kind in (0, 2, 3, 4):
            landed(w, kind, 0).wait_send()

        @pl.when(wrap)
        def _():
            landed(w, 1, 0).wait_send()


def keep(out_vmem, lse_vmem, out_hbm, lse_hbm, sem):
    copies = [
        pltpu.make_async_copy(out_vmem, out_hbm, sem.at[0]),
        pltpu.make_async_copy(lse_vmem, lse_hbm, sem.at[1]),
    ]
    for copy in copies:
        copy.start()
    for copy in copies:
        copy.wait()


def body(queries, keys, values, span_order, prev_out, earlier_log_total):
    wave = pltpu.VMEM((SLOTS + 1, 2 * SPAN, WIDTH), BF16)
    wide = pltpu.VMEM((2 * HALF, HEADS * WIDTH), BF16)
    by_row = pltpu.VMEM((2, HEADS, HALF, WIDTH), F32)
    hbm, vmem = pl.BlockSpec(memory_space=pl.ANY), pl.BlockSpec(memory_space=pltpu.VMEM)
    out, lse = pl.pallas_call(
        kernel,
        out_shape=(pltpu.VMEM(prev_out.shape, BF16), pltpu.VMEM(earlier_log_total.shape, F32)),
        in_specs=[pl.BlockSpec(memory_space=pltpu.SMEM), hbm, hbm, hbm, hbm, vmem],
        out_specs=(vmem, vmem),
        scratch_shapes=[
            *([wave] * WAVES), wide, wide,
            pltpu.VMEM((2 * SLOTS * PARTS, HEADS, HALF, SPAN), F32),
            by_row, by_row, by_row, by_row,
            pltpu.VMEM((SLOTS * PARTS, SPAN, 2 * WIDTH), BF16),
            pltpu.VMEM((2 * HALF, WIDTH), F32),
            pltpu.SemaphoreType.DMA((WAVES, 5)),
            pltpu.SemaphoreType.DMA((WAVES, 5)),
            pltpu.SemaphoreType.DMA((2,)),
        ],
        compiler_params=pltpu.CompilerParams(
            collective_id=0, has_side_effects=True, vmem_limit_bytes=57 * 1024 * 1024
        ),
        cost_estimate=pl.CostEstimate(flops=8_600_000_000, bytes_accessed=4_000_000, transcendentals=8_400_000),
        name="attend",
    )(span_order, queries, keys, values, prev_out, earlier_log_total)
    return pl.pallas_call(
        keep,
        out_shape=(
            jax.ShapeDtypeStruct(prev_out.shape, BF16),
            jax.ShapeDtypeStruct(earlier_log_total.shape, F32),
        ),
        in_specs=[vmem, vmem],
        out_specs=(hbm, hbm),
        scratch_shapes=[pltpu.SemaphoreType.DMA((2,))],
        name="keep",
    )(out, lse)


def solution(mesh):
    wide, narrow = P(("inner", "outer"), None, "head"), P(("inner", "outer"), "head", None)
    return jax.shard_map(
        body,
        mesh=mesh,
        in_specs=(wide, narrow, narrow, P(), wide, narrow),
        out_specs=(wide, narrow),
        check_vma=False,
    )
```

```python
import math

import jax
import jax.numpy as jnp
from jax import lax
from jax.experimental import pallas as pl
from jax.experimental.pallas import tpu as pltpu
from jax.sharding import PartitionSpec as P

MESH = pl.DeviceIdType.MESH
BF16, F32 = jnp.bfloat16, jnp.float32
WIDTH = 128
HALF = 512
HEADS = 4
SLOTS = 4
RELAY = 4
PIECES = 8
PARTS = 4
ROWS = WIDTH // PARTS
SPAN = HALF // PARTS
PAIR = 2 * SPAN
WAVES = 2 * PARTS
TOGETHER = 2
LOG2E = math.log2(math.e)
SCALE2 = LOG2E / math.sqrt(WIDTH)
NT = (((1,), (1,)), ((), ()))
ORDER = (0, 1, 7, 2, 6, 3, 5, 4)


def device(x, y, z, core):
    return {"head": z, "inner": (x // 2) * 2 + core, "outer": (x % 2) * 4 + y}


def kernel(
    span_ref, q_hbm, k_hbm, v_hbm, prev_hbm, lse_ref, out_ref, lse_out_ref,
    w0, w1, w2, w3, w4, w5, w6, w7, q_ref, prev_ref, scores, peak, slot_peak, carry, mixed, totals, slot_totals, va, vb, lse_cols,
    recv_sem, send_sem, local_sem,
):
    waves = (w0, w1, w2, w3, w4, w5, w6, w7)
    z, inner, outer = lax.axis_index("head"), lax.axis_index("inner"), lax.axis_index("outer")
    core = inner % 2
    x, y = (inner // 2) * 2 + outer // 4, outer % 4
    wrap = y == 0
    sibling = device(x, y, z, 1 - core)
    up = device((x + jnp.where(wrap, 1, 2)) % 4, y, z, core)
    down = device((x + 3) % 4, y, z, core)

    loads = (
        pltpu.make_async_copy(q_hbm.at[0], q_ref, local_sem.at[0]),
        pltpu.make_async_copy(prev_hbm.at[0], prev_ref, local_sem.at[1]),
    )
    for load in loads:
        load.start()

    barrier = pltpu.get_barrier_semaphore()

    def greet(to):
        pl.semaphore_signal(barrier, inc=1, device_id=to, device_id_type=MESH)

    for r in ORDER[::-1]:
        greet(device(x, (y + 3) % 4, (z + 8 - r) % 8, core))
    greet(up)
    greet(sibling)

    @pl.when(wrap)
    def _():
        greet(down)

    pl.semaphore_wait(barrier, PIECES + 2 + jnp.where(wrap, 1, 0))

    def remote(source, target, send, recv, to):
        return pltpu.make_async_remote_copy(
            src_ref=source, dst_ref=target, send_sem=send, recv_sem=recv, device_id=to, device_id_type=MESH
        )

    def landed(w, kind, slot):
        whole = waves[w].at[slot]
        return remote(whole, whole, send_sem.at[w, kind], recv_sem.at[w, kind], sibling)

    def send_out(w):
        source, part = (k_hbm, v_hbm)[w // PARTS], w % PARTS
        slot = jnp.where(y == 3, RELAY, 0)
        rows = pl.ds(pl.multiple_of(z * ROWS, ROWS), ROWS)
        for r in ORDER:
            z_to = (z + r) % 8
            columns = pl.ds(pl.multiple_of(z_to * WIDTH, WIDTH), WIDTH)
            remote(
                source.at[0, part * ROWS : (part + 1) * ROWS, columns], waves[w].at[slot, rows, :],
                send_sem.at[w, 0], recv_sem.at[w, 0], device(x, (y + 1) % 4, z_to, core),
            ).start()

    def spread(w):
        landed(w, 0, 0).wait_recv()

        @pl.when(wrap)
        def _():
            remote(waves[w].at[RELAY], waves[w].at[0], send_sem.at[w, 1], recv_sem.at[w, 1], up).start()
            remote(waves[w].at[RELAY], waves[w].at[1], send_sem.at[w, 2], recv_sem.at[w, 2], down).start()

        @pl.when(jnp.logical_not(wrap))
        def _():
            remote(waves[w].at[0], waves[w].at[1], send_sem.at[w, 2], recv_sem.at[w, 2], up).start()

    def share_first(w):
        @pl.when(wrap)
        def _():
            landed(w, 1, 0).wait_recv()

        remote(waves[w].at[0], waves[w].at[2], send_sem.at[w, 3], recv_sem.at[w, 3], sibling).start()

    def share_second(w):
        landed(w, 2, 1).wait_recv()
        remote(waves[w].at[1], waves[w].at[3], send_sem.at[w, 4], recv_sem.at[w, 4], sibling).start()

    def shared(w, slot):
        landed(w, slot + 1, slot).wait_recv()

    for w in range(WAVES):
        send_out(w)

    peak[...] = jnp.full(peak.shape, -jnp.inf, F32)
    for chunk in range(2 * HALF // WIDTH):
        half, low = chunk // 4, (chunk % 4) * WIDTH
        for h in range(HEADS):
            row = lse_ref[0, h : h + 1, chunk * WIDTH : (chunk + 1) * WIDTH] * LOG2E
            carry[half, h, low : low + WIDTH, :] = jnp.broadcast_to(row, (WIDTH, WIDTH)).T

    own_span = span_ref[inner * 8 + outer]
    first = jnp.where(wrap, (x + 3) % 4, x) // 2
    is_low = []
    for hi, at_core in ((first, core), (1 - first, core), (first, 1 - core), (1 - first, 1 - core)):
        is_low.append(span_ref[(hi * 2 + at_core) * 8 + (outer + 7) % 8] < own_span)
    loads[0].wait()

    def score(pair, slot):
        found = waves[2 * pair : 2 * pair + 2]
        low_keys = jnp.concatenate([w[slot, 0:SPAN, :] for w in found], axis=0)
        high_keys = jnp.concatenate([w[slot, SPAN : 2 * SPAN, :] for w in found], axis=0)
        either_keys = jnp.where(is_low[slot], low_keys, high_keys)
        at = (pair * SLOTS + slot) * 2
        for h in range(HEADS):
            columns = slice(h * WIDTH, (h + 1) * WIDTH)
            high = q_ref[HALF : 2 * HALF, columns]
            either = jnp.where(is_low[slot], q_ref[0:HALF, columns], high)
            tops = []
            for n, (query, key) in enumerate(((high, low_keys), (either, either_keys))):
                got = lax.dot_general(query, key, NT, preferred_element_type=F32)
                scores[at + n, h] = got
                top = got[:, 0:WIDTH]
                for low in range(WIDTH, PAIR, WIDTH):
                    top = jnp.maximum(top, got[:, low : low + WIDTH])
                tops.append(top)
            peak[0, h] = jnp.maximum(peak[0, h], jnp.where(is_low[slot], tops[1], -jnp.inf))
            peak[1, h] = jnp.maximum(
                jnp.maximum(peak[1, h], tops[0]), jnp.where(is_low[slot], -jnp.inf, tops[1])
            )

    def masked_values(parts):
        for part in parts:
            found = waves[PARTS + part]
            for slot in range(SLOTS):
                low_values, high_values = found[slot, 0:SPAN, :], found[slot, SPAN : 2 * SPAN, :]
                nothing = jnp.zeros_like(low_values)
                own = pl.ds((part * SLOTS + slot) * SPAN, SPAN)
                va[own, :] = low_values
                vb[own, 0:WIDTH] = jnp.where(is_low[slot], low_values, nothing)
                vb[own, WIDTH : 2 * WIDTH] = jnp.where(is_low[slot], nothing, high_values)

    def add(total, more):
        return more if total is None else total + more

    def mix(part, h):
        own = slice(part * SLOTS * SPAN, (part + 1) * SLOTS * SPAN)
        columns = slice((part % 2) * SPAN, (part % 2 + 1) * SPAN)
        high_total, slot_total, chunks = None, [], ([], [])
        for slot in range(SLOTS):
            at = ((part // 2) * SLOTS + slot) * 2
            weight = jnp.exp2(scores[at, h, :, columns] * SCALE2 - peak[1, h])
            high_total = add(high_total, weight)
            chunks[0].append(weight.astype(BF16))
            weight = jnp.exp2(scores[at + 1, h, :, columns] * SCALE2 - slot_peak[slot, h])
            slot_total.append(weight if part == 0 else slot_totals[slot, h] + weight)
            chunks[1].append(weight.astype(BF16))
        high_mix = jnp.dot(jnp.concatenate(chunks[0], axis=1), va[own, :], preferred_element_type=F32)
        both = jnp.dot(jnp.concatenate(chunks[1], axis=1), vb[own, :], preferred_element_type=F32)
        got = [both[:, 0:WIDTH], high_mix + both[:, WIDTH : 2 * WIDTH]]
        if part > 0:
            high_total = totals[h] + high_total
            got = [mixed[half, h] + got[half] for half in range(2)]
        return high_total, slot_total, got

    lane = lax.broadcasted_iota(jnp.int32, (HALF, WIDTH), 1)

    def mix_first(part, h):
        high_total, slot_total, got = mix(part, h)
        totals[h] = high_total
        for slot in range(SLOTS):
            slot_totals[slot, h] = slot_total[slot]
        for half in range(2):
            mixed[half, h] = got[half]

    def mix_last(part, h):
        columns = pl.ds(pl.multiple_of(h * WIDTH, WIDTH), WIDTH)
        high_total, slot_total, got = mix(part, h)
        low_total = None
        for slot in range(SLOTS):
            low_total = add(low_total, jnp.where(is_low[slot], slot_total[slot], 0.0))
            high_total = high_total + jnp.where(is_low[slot], 0.0, slot_total[slot])
        for half, total in enumerate((low_total, high_total)):
            own = slice(half * HALF, (half + 1) * HALF)
            top = peak[half, h]
            kept = jnp.exp2(carry[half, h] - top)
            total = jnp.broadcast_to(jnp.sum(total, axis=1, keepdims=True), (HALF, WIDTH)) + kept
            result = (prev_ref[own, columns].astype(F32) * kept + got[half]) / total
            out_ref[0, own, columns] = result.astype(BF16)
            log_total = top * (1.0 / LOG2E) + jnp.log(total)
            lse_cols[own, :] = jnp.where(lane == h, log_total, lse_cols[own, :])

    def heads(step, part, first, last):
        def run(n, _):
            for more in range(TOGETHER):
                step(part, TOGETHER * n + more)
            return 0

        lax.fori_loop(first // TOGETHER, last // TOGETHER, run, 0)

    def at_wrap(*steps):
        @pl.when(wrap)
        def _():
            for step, w in steps:
                step(w)

    def elsewhere(*steps):
        @pl.when(jnp.logical_not(wrap))
        def _():
            for step, w in steps:
                step(w)

    elsewhere((spread, 0), (share_first, 0), (spread, 1), (share_first, 1))
    at_wrap((spread, 0), (spread, 1), (spread, 2), (share_first, 0), (share_second, 0))
    at_wrap((spread, 3), (share_first, 1), (share_second, 1))
    score(0, 0)
    elsewhere((spread, 2), (share_first, 2), (share_second, 0), (spread, 3), (share_first, 3), (share_second, 1))
    at_wrap((spread, 4))
    score(0, 1)
    elsewhere((spread, 4), (share_first, 4))
    at_wrap((share_first, 2), (share_second, 2), (spread, 5))
    shared(0, 2)
    shared(1, 2)
    score(0, 2)
    elsewhere((share_second, 2), (spread, 5), (share_first, 5))
    at_wrap((spread, 6), (share_first, 3), (share_second, 3))
    shared(0, 3)
    shared(1, 3)
    score(0, 3)
    elsewhere((share_second, 3), (spread, 6), (share_first, 6))
    score(1, 0)
    at_wrap((spread, 7), (share_first, 4), (share_second, 4))
    score(1, 1)
    elsewhere((spread, 7), (share_first, 7), (share_second, 4))
    shared(2, 2)
    shared(3, 2)
    score(1, 2)
    at_wrap((share_first, 5), (share_second, 5))
    shared(2, 3)
    shared(3, 3)
    score(1, 3)
    elsewhere((share_second, 5))
    for half in range(2):
        for h in range(HEADS):
            top = jnp.max(peak[half, h], axis=1, keepdims=True) * SCALE2
            peak[half, h] = jnp.maximum(jnp.broadcast_to(top, (HALF, WIDTH)), carry[half, h])
    for slot in range(SLOTS):
        for h in range(HEADS):
            slot_peak[slot, h] = jnp.where(is_low[slot], peak[0, h], peak[1, h])
    at_wrap((share_first, 6), (share_second, 6))
    shared(4, 2)
    shared(4, 3)
    masked_values((0,))
    heads(mix_first, 0, 0, 2)
    elsewhere((share_second, 6))
    at_wrap((share_first, 7), (share_second, 7))
    heads(mix_first, 0, 2, HEADS)
    elsewhere((share_second, 7))
    shared(5, 2)
    shared(5, 3)
    masked_values((1,))
    heads(mix_first, 1, 0, HEADS)
    shared(6, 2)
    shared(6, 3)
    masked_values((2,))
    heads(mix_first, 2, 0, HEADS)
    shared(7, 2)
    shared(7, 3)
    masked_values((3,))
    loads[1].wait()
    lse_cols[...] = jnp.zeros(lse_cols.shape, F32)
    heads(mix_last, 3, 0, HEADS)
    for chunk in range(2 * HALF // WIDTH):
        own = slice(chunk * WIDTH, (chunk + 1) * WIDTH)
        lse_out_ref[0, :, own] = lse_cols[own, :].T[0:HEADS, :]

    for w in range(WAVES):
        for kind in (0, 2, 3, 4):
            landed(w, kind, 0).wait_send()

        @pl.when(wrap)
        def _():
            landed(w, 1, 0).wait_send()


def keep(out_vmem, lse_vmem, out_hbm, lse_hbm, sem):
    copies = [
        pltpu.make_async_copy(out_vmem, out_hbm, sem.at[0]),
        pltpu.make_async_copy(lse_vmem, lse_hbm, sem.at[1]),
    ]
    for copy in copies:
        copy.start()
    for copy in copies:
        copy.wait()


def body(queries, keys, values, span_order, prev_out, earlier_log_total):
    wave = pltpu.VMEM((SLOTS + 1, 2 * SPAN, WIDTH), BF16)
    wide = pltpu.VMEM((2 * HALF, HEADS * WIDTH), BF16)
    by_row = pltpu.VMEM((2, HEADS, HALF, WIDTH), F32)
    by_slot = pltpu.VMEM((SLOTS, HEADS, HALF, WIDTH), F32)
    by_head = pltpu.VMEM((HEADS, HALF, WIDTH), F32)
    hbm, vmem = pl.BlockSpec(memory_space=pl.ANY), pl.BlockSpec(memory_space=pltpu.VMEM)
    out, lse = pl.pallas_call(
        kernel,
        out_shape=(pltpu.VMEM(prev_out.shape, BF16), pltpu.VMEM(earlier_log_total.shape, F32)),
        in_specs=[pl.BlockSpec(memory_space=pltpu.SMEM), hbm, hbm, hbm, hbm, vmem],
        out_specs=(vmem, vmem),
        scratch_shapes=[
            *([wave] * WAVES), wide, wide,
            pltpu.VMEM((2 * SLOTS * PARTS // 2, HEADS, HALF, PAIR), F32),
            by_row, by_slot, by_row, by_row, by_head, by_slot,
            pltpu.VMEM((SLOTS * PARTS * SPAN, WIDTH), BF16),
            pltpu.VMEM((SLOTS * PARTS * SPAN, 2 * WIDTH), BF16),
            pltpu.VMEM((2 * HALF, WIDTH), F32),
            pltpu.SemaphoreType.DMA((WAVES, 5)),
            pltpu.SemaphoreType.DMA((WAVES, 5)),
            pltpu.SemaphoreType.DMA((2,)),
        ],
        compiler_params=pltpu.CompilerParams(
            collective_id=0, has_side_effects=True, vmem_limit_bytes=61 * 1024 * 1024
        ),
        cost_estimate=pl.CostEstimate(flops=8_600_000_000, bytes_accessed=4_000_000, transcendentals=8_400_000),
        name="attend",
    )(span_order, queries, keys, values, prev_out, earlier_log_total)
    return pl.pallas_call(
        keep,
        out_shape=(
            jax.ShapeDtypeStruct(prev_out.shape, BF16),
            jax.ShapeDtypeStruct(earlier_log_total.shape, F32),
        ),
        in_specs=[vmem, vmem],
        out_specs=(hbm, hbm),
        scratch_shapes=[pltpu.SemaphoreType.DMA((2,))],
        name="keep",
    )(out, lse)


def solution(mesh):
    wide, narrow = P(("inner", "outer"), None, "head"), P(("inner", "outer"), "head", None)
    return jax.shard_map(
        body,
        mesh=mesh,
        in_specs=(wide, narrow, narrow, P(), wide, narrow),
        out_specs=(wide, narrow),
        check_vma=False,
    )
```

```python
import math

import jax
import jax.numpy as jnp
from jax import lax
from jax.experimental import pallas as pl
from jax.experimental.pallas import tpu as pltpu
from jax.sharding import PartitionSpec as P

MESH = pl.DeviceIdType.MESH
BF16, F32 = jnp.bfloat16, jnp.float32
WIDTH = 128
HALF = 512
HEADS = 4
SLOTS = 4
RELAY = 4
PIECES = 8
PARTS = 4
ROWS = WIDTH // PARTS
SPAN = HALF // PARTS
PAIR = 2 * SPAN
WAVES = 2 * PARTS
TOGETHER = 2
LOG2E = math.log2(math.e)
SCALE2 = LOG2E / math.sqrt(WIDTH)
NT = (((1,), (1,)), ((), ()))
ORDER = (0, 1, 7, 2, 6, 3, 5, 4)


def device(x, y, z, core):
    return {"head": z, "inner": (x // 2) * 2 + core, "outer": (x % 2) * 4 + y}


def kernel(
    span_ref, q_hbm, k_hbm, v_hbm, prev_hbm, lse_hbm, out_ref, lse_out_ref,
    w0, w1, w2, w3, w4, w5, w6, w7, q_ref, prev_ref, scores, peak, slot_peak, carry, mixed, totals, slot_totals, va, vb, lse_cols,
    lse_ref, recv_sem, send_sem, local_sem,
):
    waves = (w0, w1, w2, w3, w4, w5, w6, w7)
    z, inner, outer = lax.axis_index("head"), lax.axis_index("inner"), lax.axis_index("outer")
    core = inner % 2
    x, y = (inner // 2) * 2 + outer // 4, outer % 4
    wrap = y == 0
    sibling = device(x, y, z, 1 - core)
    up = device((x + jnp.where(wrap, 1, 2)) % 4, y, z, core)
    down = device((x + 3) % 4, y, z, core)

    loads = (
        pltpu.make_async_copy(q_hbm.at[0], q_ref, local_sem.at[0]),
        pltpu.make_async_copy(prev_hbm.at[0], prev_ref, local_sem.at[1]),
        pltpu.make_async_copy(lse_hbm, lse_ref, local_sem.at[2]),
    )
    for load in loads:
        load.start()

    barrier = pltpu.get_barrier_semaphore()

    def greet(to):
        pl.semaphore_signal(barrier, inc=1, device_id=to, device_id_type=MESH)

    for r in ORDER[::-1]:
        greet(device(x, (y + 3) % 4, (z + 8 - r) % 8, core))
    greet(up)
    greet(sibling)

    @pl.when(wrap)
    def _():
        greet(down)

    pl.semaphore_wait(barrier, PIECES + 2 + jnp.where(wrap, 1, 0))

    def remote(source, target, send, recv, to):
        return pltpu.make_async_remote_copy(
            src_ref=source, dst_ref=target, send_sem=send, recv_sem=recv, device_id=to, device_id_type=MESH
        )

    def landed(w, kind, slot):
        whole = waves[w].at[slot]
        return remote(whole, whole, send_sem.at[w, kind], recv_sem.at[w, kind], sibling)

    def send_out(w):
        source, part = (k_hbm, v_hbm)[w // PARTS], w % PARTS
        slot = jnp.where(y == 3, RELAY, 0)
        rows = pl.ds(pl.multiple_of(z * ROWS, ROWS), ROWS)
        for r in ORDER:
            z_to = (z + r) % 8
            columns = pl.ds(pl.multiple_of(z_to * WIDTH, WIDTH), WIDTH)
            remote(
                source.at[0, part * ROWS : (part + 1) * ROWS, columns], waves[w].at[slot, rows, :],
                send_sem.at[w, 0], recv_sem.at[w, 0], device(x, (y + 1) % 4, z_to, core),
            ).start()

    def spread(w):
        landed(w, 0, 0).wait_recv()

        @pl.when(wrap)
        def _():
            remote(waves[w].at[RELAY], waves[w].at[0], send_sem.at[w, 1], recv_sem.at[w, 1], up).start()
            remote(waves[w].at[RELAY], waves[w].at[1], send_sem.at[w, 2], recv_sem.at[w, 2], down).start()

        @pl.when(jnp.logical_not(wrap))
        def _():
            remote(waves[w].at[0], waves[w].at[1], send_sem.at[w, 2], recv_sem.at[w, 2], up).start()

    def share_first(w):
        @pl.when(wrap)
        def _():
            landed(w, 1, 0).wait_recv()

        remote(waves[w].at[0], waves[w].at[2], send_sem.at[w, 3], recv_sem.at[w, 3], sibling).start()

    def share_second(w):
        landed(w, 2, 1).wait_recv()
        remote(waves[w].at[1], waves[w].at[3], send_sem.at[w, 4], recv_sem.at[w, 4], sibling).start()

    def shared(w, slot):
        landed(w, slot + 1, slot).wait_recv()

    for w in range(WAVES):
        send_out(w)

    peak[...] = jnp.full(peak.shape, -jnp.inf, F32)
    loads[2].wait()
    for chunk in range(2 * HALF // WIDTH):
        half, low = chunk // 4, (chunk % 4) * WIDTH
        for h in range(HEADS):
            row = lse_ref[0, h : h + 1, chunk * WIDTH : (chunk + 1) * WIDTH] * LOG2E
            carry[half, h, low : low + WIDTH, :] = jnp.broadcast_to(row, (WIDTH, WIDTH)).T

    own_span = span_ref[inner * 8 + outer]
    first = jnp.where(wrap, (x + 3) % 4, x) // 2
    is_low = []
    for hi, at_core in ((first, core), (1 - first, core), (first, 1 - core), (1 - first, 1 - core)):
        is_low.append(span_ref[(hi * 2 + at_core) * 8 + (outer + 7) % 8] < own_span)
    loads[0].wait()

    def score(pair, slot):
        found = waves[2 * pair : 2 * pair + 2]
        low_keys = jnp.concatenate([w[slot, 0:SPAN, :] for w in found], axis=0)
        high_keys = jnp.concatenate([w[slot, SPAN : 2 * SPAN, :] for w in found], axis=0)
        either_keys = jnp.where(is_low[slot], low_keys, high_keys)
        at = (pair * SLOTS + slot) * 2
        for h in range(HEADS):
            columns = slice(h * WIDTH, (h + 1) * WIDTH)
            high = q_ref[HALF : 2 * HALF, columns]
            either = jnp.where(is_low[slot], q_ref[0:HALF, columns], high)
            tops = []
            for n, (query, key) in enumerate(((high, low_keys), (either, either_keys))):
                got = lax.dot_general(query, key, NT, preferred_element_type=F32) * SCALE2
                scores[at + n, h] = got
                top = got[:, 0:WIDTH]
                for low in range(WIDTH, PAIR, WIDTH):
                    top = jnp.maximum(top, got[:, low : low + WIDTH])
                tops.append(top)
            peak[0, h] = jnp.maximum(peak[0, h], jnp.where(is_low[slot], tops[1], -jnp.inf))
            peak[1, h] = jnp.maximum(
                jnp.maximum(peak[1, h], tops[0]), jnp.where(is_low[slot], -jnp.inf, tops[1])
            )

    def masked_values(parts):
        for part in parts:
            found = waves[PARTS + part]
            for slot in range(SLOTS):
                low_values, high_values = found[slot, 0:SPAN, :], found[slot, SPAN : 2 * SPAN, :]
                nothing = jnp.zeros_like(low_values)
                own = pl.ds((part * SLOTS + slot) * SPAN, SPAN)
                va[own, :] = low_values
                vb[own, 0:WIDTH] = jnp.where(is_low[slot], low_values, nothing)
                vb[own, WIDTH : 2 * WIDTH] = jnp.where(is_low[slot], nothing, high_values)

    def add(total, more):
        return more if total is None else total + more

    def mix(part, h):
        own = slice(part * SLOTS * SPAN, (part + 1) * SLOTS * SPAN)
        columns = slice((part % 2) * SPAN, (part % 2 + 1) * SPAN)
        high_total, slot_total, chunks = None, [], ([], [])
        for slot in range(SLOTS):
            at = ((part // 2) * SLOTS + slot) * 2
            weight = jnp.exp2(scores[at, h, :, columns] - peak[1, h])
            high_total = add(high_total, weight)
            chunks[0].append(weight.astype(BF16))
            weight = jnp.exp2(scores[at + 1, h, :, columns] - slot_peak[slot, h])
            slot_total.append(weight if part == 0 else slot_totals[slot, h] + weight)
            chunks[1].append(weight.astype(BF16))
        high_mix = jnp.dot(jnp.concatenate(chunks[0], axis=1), va[own, :], preferred_element_type=F32)
        both = jnp.dot(jnp.concatenate(chunks[1], axis=1), vb[own, :], preferred_element_type=F32)
        got = [both[:, 0:WIDTH], high_mix + both[:, WIDTH : 2 * WIDTH]]
        if part > 0:
            high_total = totals[h] + high_total
            got = [mixed[half, h] + got[half] for half in range(2)]
        return high_total, slot_total, got

    lane = lax.broadcasted_iota(jnp.int32, (HALF, WIDTH), 1)

    def mix_first(part, h):
        high_total, slot_total, got = mix(part, h)
        totals[h] = high_total
        for slot in range(SLOTS):
            slot_totals[slot, h] = slot_total[slot]
        for half in range(2):
            mixed[half, h] = got[half]

    def mix_last(part, h):
        columns = pl.ds(pl.multiple_of(h * WIDTH, WIDTH), WIDTH)
        high_total, slot_total, got = mix(part, h)
        low_total = None
        for slot in range(SLOTS):
            low_total = add(low_total, jnp.where(is_low[slot], slot_total[slot], 0.0))
            high_total = high_total + jnp.where(is_low[slot], 0.0, slot_total[slot])
        for half, total in enumerate((low_total, high_total)):
            own = slice(half * HALF, (half + 1) * HALF)
            top = peak[half, h]
            kept = jnp.exp2(carry[half, h] - top)
            total = jnp.broadcast_to(jnp.sum(total, axis=1, keepdims=True), (HALF, WIDTH)) + kept
            result = (prev_ref[own, columns].astype(F32) * kept + got[half]) / total
            out_ref[0, own, columns] = result.astype(BF16)
            log_total = top * (1.0 / LOG2E) + jnp.log(total)
            lse_cols[own, :] = jnp.where(lane == h, log_total, lse_cols[own, :])

    def heads(step, part, first, last):
        def run(n, _):
            for more in range(TOGETHER):
                step(part, TOGETHER * n + more)
            return 0

        lax.fori_loop(first // TOGETHER, last // TOGETHER, run, 0)

    def at_wrap(*steps):
        @pl.when(wrap)
        def _():
            for step, w in steps:
                step(w)

    def elsewhere(*steps):
        @pl.when(jnp.logical_not(wrap))
        def _():
            for step, w in steps:
                step(w)

    elsewhere((spread, 0), (share_first, 0), (spread, 1), (share_first, 1))
    at_wrap((spread, 0), (spread, 1), (spread, 2), (share_first, 0), (share_second, 0))
    at_wrap((spread, 3), (share_first, 1), (share_second, 1))
    score(0, 0)
    elsewhere((spread, 2), (share_first, 2), (share_second, 0), (spread, 3), (share_first, 3), (share_second, 1))
    at_wrap((spread, 4))
    score(0, 1)
    elsewhere((spread, 4), (share_first, 4))
    at_wrap((share_first, 2), (share_second, 2), (spread, 5))
    shared(0, 2)
    shared(1, 2)
    score(0, 2)
    elsewhere((share_second, 2), (spread, 5), (share_first, 5))
    at_wrap((spread, 6), (share_first, 3), (share_second, 3))
    shared(0, 3)
    shared(1, 3)
    score(0, 3)
    elsewhere((share_second, 3), (spread, 6), (share_first, 6))
    score(1, 0)
    at_wrap((spread, 7), (share_first, 4), (share_second, 4))
    score(1, 1)
    elsewhere((spread, 7), (share_first, 7), (share_second, 4))
    shared(2, 2)
    shared(3, 2)
    score(1, 2)
    at_wrap((share_first, 5), (share_second, 5))
    shared(2, 3)
    shared(3, 3)
    score(1, 3)
    elsewhere((share_second, 5))
    for half in range(2):
        for h in range(HEADS):
            top = jnp.max(peak[half, h], axis=1, keepdims=True)
            peak[half, h] = jnp.maximum(jnp.broadcast_to(top, (HALF, WIDTH)), carry[half, h])
    for slot in range(SLOTS):
        for h in range(HEADS):
            slot_peak[slot, h] = jnp.where(is_low[slot], peak[0, h], peak[1, h])
    at_wrap((share_first, 6), (share_second, 6))
    shared(4, 2)
    shared(4, 3)
    masked_values((0,))
    heads(mix_first, 0, 0, 2)
    elsewhere((share_second, 6))
    at_wrap((share_first, 7), (share_second, 7))
    heads(mix_first, 0, 2, HEADS)
    elsewhere((share_second, 7))
    shared(5, 2)
    shared(5, 3)
    masked_values((1,))
    heads(mix_first, 1, 0, HEADS)
    shared(6, 2)
    shared(6, 3)
    masked_values((2,))
    heads(mix_first, 2, 0, HEADS)
    shared(7, 2)
    shared(7, 3)
    masked_values((3,))
    loads[1].wait()
    lse_cols[...] = jnp.zeros(lse_cols.shape, F32)
    heads(mix_last, 3, 0, HEADS)
    for chunk in range(2 * HALF // WIDTH):
        own = slice(chunk * WIDTH, (chunk + 1) * WIDTH)
        lse_out_ref[0, :, own] = lse_cols[own, :].T[0:HEADS, :]

    for w in range(WAVES):
        for kind in (0, 2, 3, 4):
            landed(w, kind, 0).wait_send()

        @pl.when(wrap)
        def _():
            landed(w, 1, 0).wait_send()


def keep(out_vmem, lse_vmem, out_hbm, lse_hbm, sem):
    copies = [
        pltpu.make_async_copy(out_vmem, out_hbm, sem.at[0]),
        pltpu.make_async_copy(lse_vmem, lse_hbm, sem.at[1]),
    ]
    for copy in copies:
        copy.start()
    for copy in copies:
        copy.wait()


def body(queries, keys, values, span_order, prev_out, earlier_log_total):
    wave = pltpu.VMEM((SLOTS + 1, 2 * SPAN, WIDTH), BF16)
    wide = pltpu.VMEM((2 * HALF, HEADS * WIDTH), BF16)
    by_row = pltpu.VMEM((2, HEADS, HALF, WIDTH), F32)
    by_slot = pltpu.VMEM((SLOTS, HEADS, HALF, WIDTH), F32)
    by_head = pltpu.VMEM((HEADS, HALF, WIDTH), F32)
    hbm, vmem = pl.BlockSpec(memory_space=pl.ANY), pl.BlockSpec(memory_space=pltpu.VMEM)
    out, lse = pl.pallas_call(
        kernel,
        out_shape=(pltpu.VMEM(prev_out.shape, BF16), pltpu.VMEM(earlier_log_total.shape, F32)),
        in_specs=[pl.BlockSpec(memory_space=pltpu.SMEM), hbm, hbm, hbm, hbm, hbm],
        out_specs=(vmem, vmem),
        scratch_shapes=[
            *([wave] * WAVES), wide, wide,
            pltpu.VMEM((2 * SLOTS * PARTS // 2, HEADS, HALF, PAIR), F32),
            by_row, by_slot, by_row, by_row, by_head, by_slot,
            pltpu.VMEM((SLOTS * PARTS * SPAN, WIDTH), BF16),
            pltpu.VMEM((SLOTS * PARTS * SPAN, 2 * WIDTH), BF16),
            pltpu.VMEM((2 * HALF, WIDTH), F32),
            pltpu.VMEM(earlier_log_total.shape, F32),
            pltpu.SemaphoreType.DMA((WAVES, 5)),
            pltpu.SemaphoreType.DMA((WAVES, 5)),
            pltpu.SemaphoreType.DMA((3,)),
        ],
        compiler_params=pltpu.CompilerParams(
            collective_id=0, has_side_effects=True, vmem_limit_bytes=61 * 1024 * 1024
        ),
        cost_estimate=pl.CostEstimate(flops=8_600_000_000, bytes_accessed=4_000_000, transcendentals=8_400_000),
        name="attend",
    )(span_order, queries, keys, values, prev_out, earlier_log_total)
    return pl.pallas_call(
        keep,
        out_shape=(
            jax.ShapeDtypeStruct(prev_out.shape, BF16),
            jax.ShapeDtypeStruct(earlier_log_total.shape, F32),
        ),
        in_specs=[vmem, vmem],
        out_specs=(hbm, hbm),
        scratch_shapes=[pltpu.SemaphoreType.DMA((2,))],
        name="keep",
    )(pltpu.with_memory_space_constraint(out, pltpu.VMEM), pltpu.with_memory_space_constraint(lse, pltpu.VMEM))


def solution(mesh):
    wide, narrow = P(("inner", "outer"), None, "head"), P(("inner", "outer"), "head", None)
    return jax.shard_map(
        body,
        mesh=mesh,
        in_specs=(wide, narrow, narrow, P(), wide, narrow),
        out_specs=(wide, narrow),
        check_vma=False,
    )
```

```python
import math

import jax
import jax.numpy as jnp
from jax import lax
from jax.experimental import pallas as pl
from jax.experimental.pallas import tpu as pltpu
from jax.sharding import PartitionSpec as P

MESH = pl.DeviceIdType.MESH
BF16, F32 = jnp.bfloat16, jnp.float32
WIDTH = 128
HALF = 512
HEADS = 4
SLOTS = 4
RELAY = 4
PIECES = 8
PARTS = 4
ROWS = WIDTH // PARTS
SPAN = HALF // PARTS
PAIR = 2 * SPAN
WAVES = 2 * PARTS
LOG2E = math.log2(math.e)
SCALE2 = LOG2E / math.sqrt(WIDTH)
NT = (((1,), (1,)), ((), ()))
ORDER = (0, 1, 7, 2, 6, 3, 5, 4)


def device(x, y, z, core):
    return {"head": z, "inner": (x // 2) * 2 + core, "outer": (x % 2) * 4 + y}


def kernel(
    span_ref, q_hbm, k_hbm, v_hbm, prev_hbm, lse_hbm, out_ref, lse_out_ref,
    w0, w1, w2, w3, w4, w5, w6, w7, q_ref, either_q, prev_ref, scores, peak, carry, mixed, totals, slot_totals, va, vb, lse_cols,
    lse_ref, recv_sem, send_sem, local_sem,
):
    waves = (w0, w1, w2, w3, w4, w5, w6, w7)
    z, inner, outer = lax.axis_index("head"), lax.axis_index("inner"), lax.axis_index("outer")
    core = inner % 2
    x, y = (inner // 2) * 2 + outer // 4, outer % 4
    wrap = y == 0
    sibling = device(x, y, z, 1 - core)
    up = device((x + jnp.where(wrap, 1, 2)) % 4, y, z, core)
    down = device((x + 3) % 4, y, z, core)

    loads = (
        pltpu.make_async_copy(q_hbm.at[0], q_ref, local_sem.at[0]),
        pltpu.make_async_copy(prev_hbm.at[0], prev_ref, local_sem.at[1]),
        pltpu.make_async_copy(lse_hbm, lse_ref, local_sem.at[2]),
    )
    for load in loads:
        load.start()

    barrier = pltpu.get_barrier_semaphore()

    def greet(to):
        pl.semaphore_signal(barrier, inc=1, device_id=to, device_id_type=MESH)

    for r in ORDER[::-1]:
        greet(device(x, (y + 3) % 4, (z + 8 - r) % 8, core))
    greet(up)
    greet(sibling)

    @pl.when(wrap)
    def _():
        greet(down)

    pl.semaphore_wait(barrier, PIECES + 2 + jnp.where(wrap, 1, 0))

    def remote(source, target, send, recv, to):
        return pltpu.make_async_remote_copy(
            src_ref=source, dst_ref=target, send_sem=send, recv_sem=recv, device_id=to, device_id_type=MESH
        )

    def landed(w, kind, slot):
        whole = waves[w].at[slot]
        return remote(whole, whole, send_sem.at[kind], recv_sem.at[w, kind], sibling)

    def send_out(w):
        source, part = (k_hbm, v_hbm)[w // PARTS], w % PARTS
        slot = jnp.where(y == 3, RELAY, 0)
        rows = pl.ds(pl.multiple_of(z * ROWS, ROWS), ROWS)
        for r in ORDER:
            z_to = (z + r) % 8
            columns = pl.ds(pl.multiple_of(z_to * WIDTH, WIDTH), WIDTH)
            remote(
                source.at[0, part * ROWS : (part + 1) * ROWS, columns], waves[w].at[slot, rows, :],
                send_sem.at[0], recv_sem.at[w, 0], device(x, (y + 1) % 4, z_to, core),
            ).start()

    def spread(w):
        landed(w, 0, 0).wait_recv()

        @pl.when(wrap)
        def _():
            remote(waves[w].at[RELAY], waves[w].at[0], send_sem.at[1], recv_sem.at[w, 1], up).start()
            remote(waves[w].at[RELAY], waves[w].at[1], send_sem.at[2], recv_sem.at[w, 2], down).start()

        @pl.when(jnp.logical_not(wrap))
        def _():
            remote(waves[w].at[0], waves[w].at[1], send_sem.at[2], recv_sem.at[w, 2], up).start()

    def share_first(w):
        @pl.when(wrap)
        def _():
            landed(w, 1, 0).wait_recv()

        remote(waves[w].at[0], waves[w].at[2], send_sem.at[3], recv_sem.at[w, 3], sibling).start()

    def share_second(w):
        landed(w, 2, 1).wait_recv()
        remote(waves[w].at[1], waves[w].at[3], send_sem.at[4], recv_sem.at[w, 4], sibling).start()

    def shared(w, slot):
        landed(w, slot + 1, slot).wait_recv()

    for w in range(WAVES):
        send_out(w)

    peak[...] = jnp.full(peak.shape, -jnp.inf, F32)
    lse_cols[...] = jnp.zeros(lse_cols.shape, F32)
    loads[2].wait()
    for chunk in range(2 * HALF // WIDTH):
        half, low = chunk // 4, (chunk % 4) * WIDTH
        for h in range(HEADS):
            row = lse_ref[0, h : h + 1, chunk * WIDTH : (chunk + 1) * WIDTH] * LOG2E
            carry[half, h, low : low + WIDTH, :] = jnp.broadcast_to(row, (WIDTH, WIDTH)).T

    own_span = span_ref[inner * 8 + outer]
    first = jnp.where(wrap, (x + 3) % 4, x) // 2
    is_low = []
    for hi, at_core in ((first, core), (1 - first, core), (first, 1 - core), (1 - first, 1 - core)):
        is_low.append(span_ref[(hi * 2 + at_core) * 8 + (outer + 7) % 8] < own_span)
    loads[0].wait()
    for slot in range(SLOTS):
        either_q[slot] = jnp.where(is_low[slot], q_ref[0:HALF, :], q_ref[HALF : 2 * HALF, :])

    def score(pair, slot):
        found = waves[2 * pair : 2 * pair + 2]
        low_keys = jnp.concatenate([w[slot, 0:SPAN, :] for w in found], axis=0)
        high_keys = jnp.concatenate([w[slot, SPAN : 2 * SPAN, :] for w in found], axis=0)
        either_keys = jnp.where(is_low[slot], low_keys, high_keys)
        at = (pair * SLOTS + slot) * 2
        for h in range(HEADS):
            columns = slice(h * WIDTH, (h + 1) * WIDTH)
            high = q_ref[HALF : 2 * HALF, columns]
            either = either_q[slot, :, columns]
            tops = []
            for n, (query, key) in enumerate(((high, low_keys), (either, either_keys))):
                got = lax.dot_general(query, key, NT, preferred_element_type=F32) * SCALE2
                scores[at + n, h] = got
                top = got[:, 0:WIDTH]
                for low in range(WIDTH, PAIR, WIDTH):
                    top = jnp.maximum(top, got[:, low : low + WIDTH])
                tops.append(top)
            peak[0, h] = jnp.maximum(peak[0, h], jnp.where(is_low[slot], tops[1], -jnp.inf))
            peak[1, h] = jnp.maximum(
                jnp.maximum(peak[1, h], tops[0]), jnp.where(is_low[slot], -jnp.inf, tops[1])
            )

    def masked_values(parts):
        for part in parts:
            found = waves[PARTS + part]
            for slot in range(SLOTS):
                low_values, high_values = found[slot, 0:SPAN, :], found[slot, SPAN : 2 * SPAN, :]
                nothing = jnp.zeros_like(low_values)
                own = pl.ds((part * SLOTS + slot) * SPAN, SPAN)
                va[own, :] = low_values
                vb[own, 0:WIDTH] = jnp.where(is_low[slot], low_values, nothing)
                vb[own, WIDTH : 2 * WIDTH] = jnp.where(is_low[slot], nothing, high_values)

    def add(total, more):
        return more if total is None else total + more

    def mix(part, h):
        own = slice(part * SLOTS * SPAN, (part + 1) * SLOTS * SPAN)
        columns = slice((part % 2) * SPAN, (part % 2 + 1) * SPAN)
        high_total, slot_total, chunks = None, [], ([], [])
        for slot in range(SLOTS):
            at = ((part // 2) * SLOTS + slot) * 2
            weight = jnp.exp2(scores[at, h, :, columns] - peak[1, h])
            high_total = add(high_total, weight)
            chunks[0].append(weight.astype(BF16))
            weight = jnp.exp2(scores[at + 1, h, :, columns] - jnp.where(is_low[slot], peak[0, h], peak[1, h]))
            slot_total.append(weight if part == 0 else slot_totals[slot, h] + weight)
            chunks[1].append(weight.astype(BF16))
        high_mix = jnp.dot(jnp.concatenate(chunks[0], axis=1), va[own, :], preferred_element_type=F32)
        both = jnp.dot(jnp.concatenate(chunks[1], axis=1), vb[own, :], preferred_element_type=F32)
        got = [both[:, 0:WIDTH], high_mix + both[:, WIDTH : 2 * WIDTH]]
        if part > 0:
            high_total = totals[h] + high_total
            got = [mixed[half, h] + got[half] for half in range(2)]
        return high_total, slot_total, got

    lane = lax.broadcasted_iota(jnp.int32, (HALF, WIDTH), 1)

    def mix_first(part, h):
        high_total, slot_total, got = mix(part, h)
        totals[h] = high_total
        for slot in range(SLOTS):
            slot_totals[slot, h] = slot_total[slot]
        for half in range(2):
            mixed[half, h] = got[half]

    def mix_last(part, h):
        columns = pl.ds(pl.multiple_of(h * WIDTH, WIDTH), WIDTH)
        high_total, slot_total, got = mix(part, h)
        low_total = None
        for slot in range(SLOTS):
            low_total = add(low_total, jnp.where(is_low[slot], slot_total[slot], 0.0))
            high_total = high_total + jnp.where(is_low[slot], 0.0, slot_total[slot])
        for half, total in enumerate((low_total, high_total)):
            own = slice(half * HALF, (half + 1) * HALF)
            top = peak[half, h]
            kept = jnp.exp2(carry[half, h] - top)
            total = jnp.broadcast_to(jnp.sum(total, axis=1, keepdims=True), (HALF, WIDTH)) + kept
            result = (prev_ref[own, columns].astype(F32) * kept + got[half]) / total
            out_ref[0, own, columns] = result.astype(BF16)
            found = jnp.where(lane == h, total, lse_cols[own, :])
            lse_cols[own, :] = jnp.where(lane == HEADS + h, top, found)

    def heads(step, part, first, last):
        def run(n, _):
            for h in range(first, last):
                step(part, h)
            return 0

        lax.fori_loop(0, 1, run, 0)

    def at_wrap(*steps):
        @pl.when(wrap)
        def _():
            for step, w in steps:
                step(w)

    def elsewhere(*steps):
        @pl.when(jnp.logical_not(wrap))
        def _():
            for step, w in steps:
                step(w)

    elsewhere((spread, 0), (share_first, 0), (spread, 1), (share_first, 1))
    at_wrap((spread, 0), (spread, 1), (spread, 2), (share_first, 0), (share_second, 0))
    at_wrap((spread, 3), (share_first, 1), (share_second, 1))
    score(0, 0)
    elsewhere((spread, 2), (share_first, 2), (share_second, 0), (spread, 3), (share_first, 3), (share_second, 1))
    at_wrap((spread, 4))
    score(0, 1)
    elsewhere((spread, 4), (share_first, 4))
    at_wrap((share_first, 2), (share_second, 2), (spread, 5))
    shared(0, 2)
    shared(1, 2)
    score(0, 2)
    elsewhere((share_second, 2), (spread, 5), (share_first, 5))
    at_wrap((spread, 6), (share_first, 3), (share_second, 3))
    shared(0, 3)
    shared(1, 3)
    score(0, 3)
    elsewhere((share_second, 3), (spread, 6), (share_first, 6))
    score(1, 0)
    at_wrap((spread, 7), (share_first, 4), (share_second, 4))
    score(1, 1)
    elsewhere((spread, 7), (share_first, 7), (share_second, 4))
    shared(2, 2)
    shared(3, 2)
    score(1, 2)
    at_wrap((share_first, 5), (share_second, 5))
    shared(2, 3)
    shared(3, 3)
    score(1, 3)
    elsewhere((share_second, 5))
    for half in range(2):
        for h in range(HEADS):
            top = jnp.max(peak[half, h], axis=1, keepdims=True)
            peak[half, h] = jnp.maximum(jnp.broadcast_to(top, (HALF, WIDTH)), carry[half, h])
    at_wrap((share_first, 6), (share_second, 6))
    shared(4, 2)
    shared(4, 3)
    masked_values((0,))
    heads(mix_first, 0, 0, 2)
    elsewhere((share_second, 6))
    at_wrap((share_first, 7), (share_second, 7))
    heads(mix_first, 0, 2, HEADS)
    elsewhere((share_second, 7))
    shared(5, 2)
    shared(5, 3)
    masked_values((1,))
    heads(mix_first, 1, 0, HEADS)
    shared(6, 2)
    shared(6, 3)
    masked_values((2,))
    heads(mix_first, 2, 0, HEADS)
    shared(7, 2)
    shared(7, 3)
    masked_values((3,))
    loads[1].wait()
    heads(mix_last, 3, 0, HEADS)
    for chunk in range(2 * HALF // WIDTH):
        own = slice(chunk * WIDTH, (chunk + 1) * WIDTH)
        found = lse_cols[own, :].T
        lse_out_ref[0, :, own] = found[HEADS : 2 * HEADS, :] * (1.0 / LOG2E) + jnp.log(found[0:HEADS, :])

    moved = scores.at[0, 0]

    def all_sent(kind):
        remote(moved, moved, send_sem.at[kind], recv_sem.at[0, 0], sibling).wait_send()

    for kind in (0, 2, 3, 4):
        all_sent(kind)

    @pl.when(wrap)
    def _():
        all_sent(1)


def keep(out_vmem, lse_vmem, out_hbm, lse_hbm, sem):
    copies = [
        pltpu.make_async_copy(out_vmem, out_hbm, sem.at[0]),
        pltpu.make_async_copy(lse_vmem, lse_hbm, sem.at[1]),
    ]
    for copy in copies:
        copy.start()
    for copy in copies:
        copy.wait()


def body(queries, keys, values, span_order, prev_out, earlier_log_total):
    wave = pltpu.VMEM((SLOTS + 1, 2 * SPAN, WIDTH), BF16)
    wide = pltpu.VMEM((2 * HALF, HEADS * WIDTH), BF16)
    by_row = pltpu.VMEM((2, HEADS, HALF, WIDTH), F32)
    by_slot = pltpu.VMEM((SLOTS, HEADS, HALF, WIDTH), F32)
    by_head = pltpu.VMEM((HEADS, HALF, WIDTH), F32)
    hbm, vmem = pl.BlockSpec(memory_space=pl.ANY), pl.BlockSpec(memory_space=pltpu.VMEM)
    out, lse = pl.pallas_call(
        kernel,
        out_shape=(pltpu.VMEM(prev_out.shape, BF16), pltpu.VMEM(earlier_log_total.shape, F32)),
        in_specs=[pl.BlockSpec(memory_space=pltpu.SMEM), hbm, hbm, hbm, hbm, hbm],
        out_specs=(vmem, vmem),
        scratch_shapes=[
            *([wave] * WAVES), wide,
            pltpu.VMEM((SLOTS, HALF, HEADS * WIDTH), BF16),
            wide,
            pltpu.VMEM((2 * SLOTS * PARTS // 2, HEADS, HALF, PAIR), F32),
            by_row, by_row, by_row, by_head, by_slot,
            pltpu.VMEM((SLOTS * PARTS * SPAN, WIDTH), BF16),
            pltpu.VMEM((SLOTS * PARTS * SPAN, 2 * WIDTH), BF16),
            pltpu.VMEM((2 * HALF, WIDTH), F32),
            pltpu.VMEM(earlier_log_total.shape, F32),
            pltpu.SemaphoreType.DMA((WAVES, 5)),
            pltpu.SemaphoreType.DMA((5,)),
            pltpu.SemaphoreType.DMA((3,)),
        ],
        compiler_params=pltpu.CompilerParams(
            collective_id=0, has_side_effects=True, vmem_limit_bytes=61 * 1024 * 1024
        ),
        cost_estimate=pl.CostEstimate(flops=8_600_000_000, bytes_accessed=4_000_000, transcendentals=8_400_000),
        name="attend",
    )(span_order, queries, keys, values, prev_out, earlier_log_total)
    return pl.pallas_call(
        keep,
        out_shape=(
            jax.ShapeDtypeStruct(prev_out.shape, BF16),
            jax.ShapeDtypeStruct(earlier_log_total.shape, F32),
        ),
        in_specs=[vmem, vmem],
        out_specs=(hbm, hbm),
        scratch_shapes=[pltpu.SemaphoreType.DMA((2,))],
        name="keep",
    )(pltpu.with_memory_space_constraint(out, pltpu.VMEM), pltpu.with_memory_space_constraint(lse, pltpu.VMEM))


def solution(mesh):
    wide, narrow = P(("inner", "outer"), None, "head"), P(("inner", "outer"), "head", None)
    return jax.shard_map(
        body,
        mesh=mesh,
        in_specs=(wide, narrow, narrow, P(), wide, narrow),
        out_specs=(wide, narrow),
        check_vma=False,
    )
```
